128 devices in a mesh: seq: 16 (over x, y_lo, core), grp: 8 (over y_hi, z).
Axes of the slice: x: 4, y: 4 (y_hi: 2, y_lo: 2; y = y_hi * 2 + y_lo), z: 4, core: 2. Of those that a mesh axis runs over, the one named last changes fastest.
Arguments:
- prompt: bfloat16 [16384, 4096], P('seq'), may hold values from -6 to 6
- w_query: bfloat16 [4096, 4096], P(None, 'grp'), may hold values from -0.09375 to 0.09375
- key_weight: bfloat16 [4096, 1024], P(None, 'grp'), may hold values from -0.09375 to 0.09375
- value_weight: bfloat16 [4096, 1024], P(None, 'grp'), may hold values from -0.09375 to 0.09375
- q_gain: float32 [128], replicated, may hold values from 0.5 to 16
- key_norm_gain: float32 [128], replicated, may hold values from 0.5 to 16
- block_mask: int32 [32, 32], replicated, may hold values from 0 to 1, as said below
- continuation_tokens: bfloat16 [4, 256, 4096], P(None, 'seq'), may hold values from -6 to 6
- row_map: int32 [256], replicated, may hold values from 0 to 255, each once
Outputs:
- prefill_out: bfloat16 [16384, 4096], P('seq', 'grp')
- decode_out: bfloat16 [4, 256, 4096], P(None, 'grp', 'seq')
The draws below stay inside these ranges and needn't reach their ends.
Inputs may be any that keep to these rules, and one draw needn't show every extreme that they name: `block_mask`: entries on the diagonal are 1 and above it 0; entries below it are 0 or 1. `row_map`: each continuation row appears in exactly one slot.
All inputs are finite; a program needn't handle non-finite values.
Results may differ from the reference program's by a relative error of at most 0.02.
The reference program's roundings to bfloat16 on the way count: a program that leaves them out, or rounds other values in their place, can miss the bound.
Values may be sent and summed in bfloat16 or wider, within the bound.
A program may use at most 192 MiB of HBM per device.

```python
import math
import jax
import jax.numpy as jnp
from jax import lax

MODEL_WIDTH = 4096
QUERY_HEADS = 32
KEY_VALUE_HEADS = 8
HEAD_SIZE = 128
BLK = 512
STEPS = 4
PROMPT = 16384
NBLK = 32
ROWS = 256


def draw_block_mask(key, part):
    key = jax.random.fold_in(key, 7)
    coins = jax.random.randint(key, (NBLK, NBLK), 0, 2)
    row_ids = jnp.arange(NBLK)[:, None]
    column_ids = jnp.arange(NBLK)[None, :]
    return jnp.where(row_ids == column_ids, 1, jnp.where(column_ids < row_ids, coins, 0)).astype(jnp.int32)


def chosen_pairs(key):
    shared_key = jax.random.fold_in(key, 101)
    picks = jax.random.randint(shared_key, (HEAD_SIZE // 2,), 0, 4)
    pair_ids = jnp.arange(HEAD_SIZE // 2)
    chosen = (picks == 0) & (pair_ids >= 3 * HEAD_SIZE // 8) | (pair_ids == HEAD_SIZE // 2 - 1)
    return jnp.concatenate([chosen, chosen])


def gain_values(key, chosen, strong_lo, strong_hi):
    drawn_key, strong_key = jax.random.split(key)
    drawn = jax.random.uniform(drawn_key, (HEAD_SIZE,), jnp.float32, 0.5, 2.0)
    strong = jax.random.uniform(strong_key, (HEAD_SIZE,), jnp.float32, strong_lo, strong_hi)
    last_pair = jnp.arange(HEAD_SIZE) % (HEAD_SIZE // 2) == HEAD_SIZE // 2 - 1
    strong = jnp.where(last_pair, strong_hi, strong)
    return jnp.where(chosen, strong, drawn).astype(jnp.float32)


def draw_q_gain(key, part):
    chosen = chosen_pairs(key)
    key = jax.random.fold_in(key, 11)
    return gain_values(key, chosen, 2.0, 3.0)


def draw_key_norm_gain(key, part):
    chosen = chosen_pairs(key)
    key = jax.random.fold_in(key, 13)
    return gain_values(key, chosen, 2.0, 3.0)


def levels(stream_key, extent, shards, least, largest):
    gain, own = 1.0, jax.random.fold_in(stream_key, 6)
    for position, parts in shards:
        draws = jnp.exp(jax.random.uniform(jax.random.fold_in(own, position), (parts,), jnp.float32, least / len(shards), largest / len(shards)))
        gain = gain * jnp.repeat(draws, extent[position] // parts).reshape([-1 if axis == position else 1 for axis in range(len(extent))])
    return gain


def centred(stream_key, shape, spread, most, pieces=(), held_as=jnp.bfloat16):
    drawn = spread * jax.random.normal(stream_key, shape, jnp.float32)
    if pieces:
        drawn = drawn * levels(stream_key, shape, pieces, -0.22, 0.18)
    return jnp.clip(drawn, -most, most).astype(held_as)


def setup_inputs(seed: int = 0) -> dict:
    keys = jax.random.split(jax.random.key(seed), 10)
    return {
        "prompt": centred(keys[0], (PROMPT, MODEL_WIDTH), 1.0, 6.0, ((0, 16),)),
        "w_query": centred(keys[1], (MODEL_WIDTH, QUERY_HEADS * HEAD_SIZE), MODEL_WIDTH ** -0.5, 0.09375, ((1, 8),)),
        "key_weight": centred(keys[2], (MODEL_WIDTH, KEY_VALUE_HEADS * HEAD_SIZE), MODEL_WIDTH ** -0.5, 0.09375, ((1, 8),)),
        "value_weight": centred(keys[3], (MODEL_WIDTH, KEY_VALUE_HEADS * HEAD_SIZE), MODEL_WIDTH ** -0.5, 0.09375, ((1, 8),)),
        "q_gain": draw_q_gain(jax.random.fold_in(keys[9], 71), 0),
        "key_norm_gain": draw_key_norm_gain(jax.random.fold_in(keys[9], 71), 0),
        "block_mask": draw_block_mask(jax.random.fold_in(keys[9], 71), 0),
        "continuation_tokens": centred(keys[7], (STEPS, ROWS, MODEL_WIDTH), 1.0, 6.0, ((1, 16),)),
        "row_map": jax.random.permutation(keys[8], ROWS).astype(jnp.int32),
    }


ROPE_BASE = 1000000.0
NORM_EPS = 1e-06
MASKED_SCORE = -1e+30

def rope_tables(positions, head_width):
    half_width = head_width // 2
    frequency = ROPE_BASE ** (-jnp.arange(half_width, dtype=jnp.float32) * (2.0 / head_width))
    angles = positions.astype(jnp.float32)[:, None] * frequency[None, :]
    return (jnp.cos(angles), jnp.sin(angles))

def rotate_half(vectors, cosine_lookup, sine_lookup):
    half_width = vectors.shape[-1] // 2
    lower_half = vectors[..., :half_width]
    upper_half = vectors[..., half_width:]
    return jnp.concatenate([lower_half * cosine_lookup - upper_half * sine_lookup, upper_half * cosine_lookup + lower_half * sine_lookup], axis=-1)

def head_projector(inputs, weight, head_count, head_gain, cosine_lookup, sine_lookup):
    flat_inputs = inputs.reshape(-1, inputs.shape[-1])
    projected = jnp.dot(flat_inputs, weight, preferred_element_type=jnp.float32)
    projected = projected.reshape(inputs.shape[:-1] + (head_count, weight.shape[1] // head_count))
    normed = projected * lax.rsqrt(lax.optimization_barrier(jnp.mean(projected * projected, axis=-1, keepdims=True)) + NORM_EPS) * head_gain
    return rotate_half(normed, cosine_lookup, sine_lookup).astype(jnp.bfloat16)

def rounded_weights(weights):
    narrow = weights.astype(jnp.bfloat16)
    narrow = lax.optimization_barrier(narrow)
    return narrow.astype(jnp.float32)

def reference(prompt, w_query, key_weight, value_weight, q_gain, key_norm_gain, block_mask, continuation_tokens, row_map):
    sequence_length = prompt.shape[0]
    group_members = QUERY_HEADS // KEY_VALUE_HEADS
    score_scale = 1.0 / math.sqrt(HEAD_SIZE)
    cosine_lookup, sine_lookup = rope_tables(jnp.arange(sequence_length), HEAD_SIZE)
    query_vector = head_projector(prompt, w_query, QUERY_HEADS, q_gain, cosine_lookup[:, None, :], sine_lookup[:, None, :])
    key_row_block = head_projector(prompt, key_weight, KEY_VALUE_HEADS, key_norm_gain, cosine_lookup[:, None, :], sine_lookup[:, None, :])
    value_row_block = jnp.dot(prompt, value_weight, preferred_element_type=jnp.float32).astype(jnp.bfloat16).reshape(sequence_length, KEY_VALUE_HEADS, HEAD_SIZE)
    key_heads = jnp.transpose(key_row_block, (1, 0, 2)).astype(jnp.float32)
    value_heads = jnp.transpose(value_row_block, (1, 0, 2)).astype(jnp.float32)
    query_head_rows = jnp.transpose(query_vector.reshape(sequence_length, KEY_VALUE_HEADS, group_members, HEAD_SIZE), (1, 2, 0, 3))
    token_block = jnp.arange(sequence_length) // BLK
    blocks_seen = block_mask > 0
    key_positions = jnp.arange(sequence_length)

    def prefill_block(block_index):
        first_row = block_index * BLK
        visible_keys = blocks_seen[block_index][token_block]
        query_positions = first_row + jnp.arange(BLK)
        visible = visible_keys[None, :] & (key_positions[None, :] <= query_positions[:, None])

        def single_head(head_index):
            head_query = lax.dynamic_slice_in_dim(query_head_rows[head_index], first_row, BLK, 1).astype(jnp.float32)
            scores = jnp.einsum('gqd,sd->gqs', head_query, key_heads[head_index]) * score_scale
            scores = jnp.where(visible[None], scores, MASKED_SCORE)
            highest = lax.optimization_barrier(jnp.max(scores, axis=-1, keepdims=True))
            weights = jnp.where(visible[None], jnp.exp(scores - highest), 0.0)
            weight_sum = lax.optimization_barrier(jnp.sum(weights, axis=-1, keepdims=True))
            combined = jnp.einsum('gqs,sd->gqd', rounded_weights(weights), value_heads[head_index])
            return combined / weight_sum
        block_output = lax.map(single_head, jnp.arange(KEY_VALUE_HEADS))
        return jnp.transpose(block_output, (2, 0, 1, 3)).reshape(BLK, QUERY_HEADS * HEAD_SIZE).astype(jnp.bfloat16)
    prefill_out = lax.map(prefill_block, jnp.arange(sequence_length // BLK)).reshape(sequence_length, QUERY_HEADS * HEAD_SIZE)
    decode_step_count = continuation_tokens.shape[0]
    decode_cosine_row, decode_sine_row = rope_tables(sequence_length + jnp.arange(decode_step_count), HEAD_SIZE)
    step_query = head_projector(continuation_tokens, w_query, QUERY_HEADS, q_gain, decode_cosine_row[:, None, None, :], decode_sine_row[:, None, None, :])
    step_key_row = head_projector(continuation_tokens, key_weight, KEY_VALUE_HEADS, key_norm_gain, decode_cosine_row[:, None, None, :], decode_sine_row[:, None, None, :])
    step_value_row = jnp.dot(continuation_tokens.reshape(-1, continuation_tokens.shape[2]), value_weight, preferred_element_type=jnp.float32).astype(jnp.bfloat16)
    step_value_row = step_value_row.reshape(decode_step_count, continuation_tokens.shape[1], KEY_VALUE_HEADS, HEAD_SIZE)
    step_query = jnp.take(step_query, row_map, axis=1)
    step_key_row = jnp.take(step_key_row, row_map, axis=1)
    step_value_row = jnp.take(step_value_row, row_map, axis=1)
    step_order = jnp.arange(decode_step_count)[None, :] <= jnp.arange(decode_step_count)[:, None]
    own_mask = step_order[:, None, None, :]

    def decode_single_head(head_index):
        head_query = lax.dynamic_slice_in_dim(step_query, head_index * group_members, group_members, 2).astype(jnp.float32)
        prompt_scores = jnp.einsum('trgd,sd->trgs', head_query, key_heads[head_index]) * score_scale
        own_keys = step_key_row[:, :, head_index].astype(jnp.float32)
        own_values = step_value_row[:, :, head_index].astype(jnp.float32)
        own_scores = jnp.einsum('trgd,urd->trgu', head_query, own_keys) * score_scale
        own_scores = jnp.where(own_mask, own_scores, MASKED_SCORE)
        highest = jnp.maximum(lax.optimization_barrier(jnp.max(prompt_scores, axis=-1)), lax.optimization_barrier(jnp.max(own_scores, axis=-1)))[..., None]
        prompt_weights = jnp.exp(prompt_scores - highest)
        own_weights = jnp.where(own_mask, jnp.exp(own_scores - highest), 0.0)
        weight_sum = lax.optimization_barrier(jnp.sum(prompt_weights, axis=-1)) + lax.optimization_barrier(jnp.sum(own_weights, axis=-1))
        combined = jnp.einsum('trgs,sd->trgd', rounded_weights(prompt_weights), value_heads[head_index])
        combined = combined + jnp.einsum('trgu,urd->trgd', rounded_weights(own_weights), own_values)
        return combined / weight_sum[..., None]
    decode_every_head = lax.map(decode_single_head, jnp.arange(KEY_VALUE_HEADS))
    row_total = row_map.shape[0]
    decode_out = jnp.transpose(decode_every_head, (1, 2, 0, 3, 4)).reshape(decode_step_count, row_total, QUERY_HEADS * HEAD_SIZE).astype(jnp.bfloat16)
    return (prefill_out, decode_out)
```

```python
import functools
import math

import jax
import jax.numpy as jnp
from jax import lax
from jax.experimental import pallas as pl
from jax.experimental.pallas import tpu as pltpu
from jax.sharding import PartitionSpec as P

HEADS = 4
D = 128
BLK = 512
ROPE_BASE = 1000000.0
NORM_EPS = 1e-06
SCALE = math.log2(math.e) / math.sqrt(D)
MASKED = -1e30
MESH = pl.DeviceIdType.MESH
F32, BF16 = jnp.float32, jnp.bfloat16


def rope_tables(positions):
    frequency = ROPE_BASE ** (-jnp.arange(D // 2, dtype=F32) * (2.0 / D))
    angles = positions.astype(F32)[:, None] * frequency[None, :]
    return jnp.concatenate([jnp.cos(angles), jnp.sin(angles)], axis=-1)


def both_halves(table):
    turned = pltpu.roll(table, D // 2, 1)
    low = lax.broadcasted_iota(jnp.int32, table.shape, 1) < D // 2
    return jnp.where(low, table, turned), jnp.where(low, -turned, table)


def norm_rope(u, gain, cosine, sine):
    normed = u * lax.rsqrt(jnp.mean(u * u, axis=-1, keepdims=True) + NORM_EPS) * gain
    return (normed * cosine + pltpu.roll(normed, D // 2, 1) * sine).astype(BF16)


def matmul(a, b):
    return lax.dot_general(a, b, (((1,), (0,)), ((), ())), preferred_element_type=F32)


def matmul_nt(a, b):
    return lax.dot_general(a, b, (((1,), (1,)), ((), ())), preferred_element_type=F32)


def front_kernel(
    x_any, wq_any, wk_any, wv_any, tok_any, qg_ref, kg_ref, table_ref, ttable_ref, map_ref,
    q_ref, m, l, a, decode_ref, k_out, vt_out,
    x, wq, wkv, tok, k, vt, tq, tm, tl, ta, rows_out, arriving, tall, load_sems, send_sems, recv_sems, store_sems,
    out_sems, in_sems,
):
    me, grp = lax.axis_index("seq"), lax.axis_index("grp")
    right, left = lax.rem(me + 4, 16), lax.rem(me + 12, 16)
    y = me + 2 - 4 * lax.rem(me // 2, 2)
    other_core = lambda s: s + 1 - 2 * lax.rem(s, 2)
    core = other_core(me)
    yright, yleft = lax.rem(y + 4, 16), lax.rem(y + 12, 16)
    far, yfar = lax.rem(me + 8, 16), lax.rem(y + 8, 16)
    barrier = pltpu.get_barrier_semaphore()
    for n in (right, left, y, core):
        pl.semaphore_signal(barrier, inc=1, device_id=(n, grp), device_id_type=MESH)
    home = me // 2
    at_home = home == grp

    def is_me(c):
        return at_home & (2 * grp + c == me)

    for c in (0, 1):

        @pl.when(jnp.logical_not(is_me(c)))
        def _():
            pl.semaphore_signal(barrier, inc=1, device_id=(2 * grp + c, home), device_id_type=MESH)

    pairs = [(wk_any, wkv.at[:, :D]), (wv_any, wkv.at[:, D:])]
    pairs += [(tok_any, tok), (wq_any, wq)]
    pairs += [(x_any.at[pl.ds(h * BLK, BLK)], x.at[pl.ds(h * BLK, BLK)]) for h in (0, 1)]
    loads = [pltpu.make_async_copy(src, dst, load_sems.at[i]) for i, (src, dst) in enumerate(pairs)]
    for c in loads:
        c.start()

    sends = []
    outs = (k, vt, tall)
    K, V, T = 0, 1, 2

    def remote(kind, chunk, half, send_sem, to):
        block = outs[kind].at[2 * chunk + half]
        return pltpu.make_async_remote_copy(
            src_ref=block, dst_ref=block, send_sem=send_sem, recv_sem=recv_sems.at[kind, chunk, half],
            device_id=(to, grp), device_id_type=MESH,
        )

    def send(kind, chunk, half, to):
        c = remote(kind, chunk, half, send_sems.at[len(sends)], to)
        c.start()
        sends.append(c)

    def arrived(kind, chunk, half):
        remote(kind, chunk, half, send_sems.at[0], core).wait_recv()

    def forward(kind, chunk, half, *to):
        arrived(kind, chunk, half)
        for t in to:
            send(kind, chunk, half, t)

    n_tok = tok.shape[0]
    steps = 4
    per = n_tok // steps
    for c in loads[:4]:
        c.wait()
    cosine, sine = both_halves(ttable_ref[...])
    kv = matmul(tok[...], wkv[...])
    q = matmul(tok[...], wq[...])
    mixed = [norm_rope(q[:, h * D : (h + 1) * D], qg_ref[...], cosine, sine) for h in range(HEADS)]
    mixed += [norm_rope(kv[:, :D], kg_ref[...], cosine, sine), kv[:, D:].astype(BF16)]
    mixed = jnp.concatenate(mixed, axis=1)
    for h in (0, 1):
        tall[2 * me + h] = mixed[h * n_tok // 2 : (h + 1) * n_tok // 2]
    pl.semaphore_wait(barrier, 6 - jnp.where(at_home, 1, 0))
    for h in (0, 1):
        for to in (y, right, left, core):
            send(T, me, h, to)
    for h in (0, 1):
        loads[4 + h].wait()
        rows = slice(h * BLK, (h + 1) * BLK)
        kv = matmul(x[rows, :], wkv[...])
        cosine, sine = both_halves(table_ref[rows, :])
        k[2 * me + h] = norm_rope(kv[:, :D], kg_ref[...], cosine, sine)
        vt[2 * me + h] = kv[:, D:].T.astype(BF16)
        send(V, me, h, y)
        send(K, me, h, right)
        send(K, me, h, left)
        send(K, me, h, y)
        send(V, me, h, right)
        send(V, me, h, left)
        send(K, me, h, core)
        send(V, me, h, core)

    def query_tile(i):
        rows = slice(i * 256, (i + 1) * 256)
        cosine, sine = both_halves(table_ref[rows, :])
        q = matmul(x[rows, :], wq[...])
        for h in range(HEADS):
            cols = slice(h * D, (h + 1) * D)
            q_ref[rows, cols] = norm_rope(q[:, cols], qg_ref[...], cosine, sine)

    def slots():
        shape = (n_tok, map_ref.shape[1])
        slot = me * per + lax.broadcasted_iota(jnp.int32, shape, 0) % per
        mine = lax.broadcasted_iota(jnp.int32, shape, 1) == slot
        row = jnp.sum(jnp.where(mine, map_ref[...].astype(F32), 0.0), axis=1, keepdims=True).astype(jnp.int32)
        source = (row >> 4) * n_tok + lax.broadcasted_iota(jnp.int32, (n_tok, 1), 0) // per * per + (row & 15)
        shape = (n_tok, 16 * n_tok)
        picked = jnp.where(lax.broadcasted_iota(jnp.int32, shape, 1) == source, 1.0, 0.0).astype(BF16)
        mixed = matmul(picked, tall[...].reshape(16 * n_tok, (HEADS + 2) * D))
        for h in range(HEADS):
            tq[h * n_tok : (h + 1) * n_tok, :] = mixed[:, h * D : (h + 1) * D].astype(BF16)
        tk = mixed[:, HEADS * D : (HEADS + 1) * D].astype(BF16)
        tvt = mixed[:, (HEADS + 1) * D :].T.astype(BF16)
        own = matmul_nt(tk, tq[...])
        key_id = lax.broadcasted_iota(jnp.int32, own.shape, 0)
        row_id = lax.broadcasted_iota(jnp.int32, own.shape, 1) % n_tok
        seen = (key_id % per == row_id % per) & (key_id // per <= row_id // per)
        first_part(jnp.where(seen, own, MASKED), tvt, tm, tl, ta)

    def diagonal(b):
        shape = (BLK, BLK)
        causal = lax.broadcasted_iota(jnp.int32, shape, 0) <= lax.broadcasted_iota(jnp.int32, shape, 1)
        for h in range(HEADS):
            s = matmul_nt(k[2 * me + b], q_ref[b * BLK : (b + 1) * BLK, h * D : (h + 1) * D])
            first_part(jnp.where(causal, s, MASKED), vt[2 * me + b], m.at[b, h], l.at[b, h], a.at[b, h])

    def store(chunk, i):
        two = pl.ds(2 * chunk, 2)
        return [
            pltpu.make_async_copy(k.at[two], k_out.at[two], store_sems.at[0, i]),
            pltpu.make_async_copy(vt.at[two], vt_out.at[two], store_sems.at[1, i]),
        ]

    def chunk_of(base, dx, c):
        mine = lax.rem(base + 4 * dx, 16)
        return mine if c == 0 else other_core(mine)

    def decode(base, first):
        def step(dx, carry):
            here, there = chunk_of(base, dx, 0), chunk_of(base, dx, 1)
            for kind in (K, V):
                for h in (0, 1):
                    arrived(kind, there, h)
            scores = [
                matmul_nt(jnp.concatenate([k[2 * c], k[2 * c + 1]], axis=0), tq[...]) for c in (here, there)
            ]
            for s, c, i in zip(scores, (here, there), (0, 1)):
                for copy in store(c, first + 2 * dx + i):
                    copy.start()
                next_part(s, jnp.concatenate([vt[2 * c], vt[2 * c + 1]], axis=1), tm, tl, ta)
            return carry

        lax.fori_loop(0, 4, step, 0)

    for h in (0, 1):
        forward(T, y, h, right, left, core)
    forward(T, left, 0, right, core)
    forward(T, right, 1, left, core)
    forward(K, left, 0, right, y, core)
    forward(K, right, 0, y, core)
    for h in (0, 1):
        forward(V, y, h, right, left, core)
    forward(T, left, 1, core)
    forward(T, right, 0, core)
    forward(T, yleft, 0, right, core)
    forward(T, yright, 1, left, core)
    query_tile(0)
    forward(K, right, 1, left, y, core)
    forward(K, left, 1, y, core)
    forward(V, left, 0, right, core)
    forward(T, yleft, 1, core)
    forward(T, yright, 0, core)
    for h in (0, 1):
        forward(T, far, h, core)
    query_tile(1)
    forward(V, right, 0, core)
    forward(V, right, 1, left, core)
    forward(V, left, 1, core)
    for h in (0, 1):
        forward(T, yfar, h, core)
    query_tile(2)
    for h in (0, 1):
        forward(K, y, h, core)
    forward(K, far, 0, y, core)
    query_tile(3)
    for chunk in (me, y, left, right, far, yleft, yright, yfar):
        for h in (0, 1):
            arrived(T, other_core(chunk), h)
    slots()
    forward(K, far, 1, y, core)
    forward(V, yleft, 0, right, core)
    forward(V, yright, 1, left, core)
    for h in (0, 1):
        forward(V, far, h, core)
    for h in (0, 1):
        forward(K, yleft, h, core)
        forward(K, yright, 1 - h, core)
    forward(V, yleft, 1, core)
    forward(V, yright, 0, core)
    decode(me, 0)
    for h in (0, 1):
        forward(K, yfar, h, core)
        forward(V, yfar, h, core)
    decode(y, 8)
    out = (ta[...] / tl[...]).T.astype(BF16)
    for c in (0, 1):
        for h in (0, 1):
            rows = slice((2 * c + h) * n_tok, (2 * c + h + 1) * n_tok)
            rows_out[c, :, h * D : (h + 1) * D] = out[rows, :]

    def place(c):
        here = arriving.at[lax.rem(me, 2)]
        local = pltpu.make_async_copy(rows_out.at[c], here, out_sems.at[c])
        away = pltpu.make_async_remote_copy(
            src_ref=rows_out.at[c], dst_ref=here, send_sem=out_sems.at[c], recv_sem=in_sems.at[lax.rem(me, 2)],
            device_id=(2 * grp + c, home), device_id_type=MESH,
        )
        return local, away

    for c in (0, 1):
        local, away = place(c)
        pl.when(is_me(c))(local.start)
        pl.when(jnp.logical_not(is_me(c)))(away.start)
    diagonal(0)
    diagonal(1)
    for c in (0, 1):
        local, away = place(c)
        pl.when(is_me(c))(local.wait)
        pl.when(jnp.logical_not(is_me(c)))(away.wait_send)
        there = pltpu.make_async_remote_copy(
            src_ref=arriving.at[c], dst_ref=arriving.at[c], send_sem=out_sems.at[c], recv_sem=in_sems.at[c],
            device_id=(core, grp), device_id_type=MESH,
        )
        pl.when(jnp.logical_not(is_me(c)))(there.wait_recv)
    for t in range(steps):
        for c in (0, 1):
            decode_ref[t, c * per : (c + 1) * per, :] = arriving[c, t * per : (t + 1) * per, :]
    for c in sends:
        c.wait_send()
    for base, first in ((me, 0), (y, 8)):

        def finish(dx, carry):
            for i in (0, 1):
                for copy in store(chunk_of(base, dx, i), first + 2 * dx + i):
                    copy.wait()
            return carry

        lax.fori_loop(0, 4, finish, 0)


def front(x, wq, wk, wv, tok, qg, kg, table, ttable, row_map):
    rows, width = x.shape
    n_tok = tok.shape[0]
    vmem = pl.BlockSpec(memory_space=pltpu.VMEM)
    anywhere = pl.BlockSpec(memory_space=pl.ANY)
    dma = pltpu.SemaphoreType.DMA
    return pl.pallas_call(
        front_kernel,
        out_shape=[
            jax.ShapeDtypeStruct((rows, HEADS * D), BF16),
            jax.ShapeDtypeStruct((2, HEADS, 1, BLK), F32),
            jax.ShapeDtypeStruct((2, HEADS, 1, BLK), F32),
            jax.ShapeDtypeStruct((2, HEADS, D, BLK), F32),
            jax.ShapeDtypeStruct((4, n_tok // 2, 2 * D), BF16),
            jax.ShapeDtypeStruct((32, BLK, D), BF16),
            jax.ShapeDtypeStruct((32, D, BLK), BF16),
        ],
        in_specs=[anywhere] * 5 + [vmem] * 5,
        out_specs=[vmem] * 5 + [anywhere] * 2,
        scratch_shapes=[
            pltpu.VMEM((rows, width), BF16),
            pltpu.VMEM((width, HEADS * D), BF16),
            pltpu.VMEM((width, 2 * D), BF16),
            pltpu.VMEM((n_tok, width), BF16),
            pltpu.VMEM((32, BLK, D), BF16),
            pltpu.VMEM((32, D, BLK), BF16),
            pltpu.VMEM((HEADS * n_tok, D), BF16),
            pltpu.VMEM((1, HEADS * n_tok), F32),
            pltpu.VMEM((1, HEADS * n_tok), F32),
            pltpu.VMEM((D, HEADS * n_tok), F32),
            pltpu.VMEM((2, n_tok, 2 * D), BF16),
            pltpu.VMEM((2, n_tok, 2 * D), BF16),
            pltpu.VMEM((32, n_tok // 2, (HEADS + 2) * D), BF16),
            dma((6,)),
            dma((96,)),
            dma((3, 16, 2)),
            dma((2, 16)),
            dma((2,)),
            dma((2,)),
        ],
        compiler_params=pltpu.CompilerParams(
            collective_id=0, has_side_effects=True, vmem_limit_bytes=56 << 20
        ),
        name="front",
    )(x, wq, wk, wv, tok, qg, kg, table, ttable, row_map)


def first_part(s, vt, m, l, a):
    top = jnp.max(s, axis=0, keepdims=True)
    p = jnp.exp2((s - top) * SCALE)
    m[...] = top
    l[...] = jnp.sum(p, axis=0, keepdims=True)
    a[...] = matmul(vt, p.astype(BF16))


def next_part(s, vt, m, l, a):
    before = m[...]
    top = jnp.maximum(before, jnp.max(s, axis=0, keepdims=True))
    p = jnp.exp2(s * SCALE - top * SCALE)
    keep = jnp.exp2((before - top) * SCALE)
    l[...] = l[...] * keep + jnp.sum(p, axis=0, keepdims=True)
    a[...] = a[...] * keep + matmul(vt, p.astype(BF16))
    m[...] = top


def prefill_block(here, mask, listed, q, m, l, a, k, vt, ahead, fetch, have):
    listed[0] = 0

    def note(j, n):
        listed[n] = j
        return n + jnp.where(mask[here, j] > 0, 1, 0)

    count = lax.fori_loop(0, here, note, 0)
    twos = count // 2

    def scores(i, h):
        keys = jnp.concatenate([k[listed[2 * i]], k[listed[2 * i + 1]]], axis=0)
        return matmul_nt(keys, q(h))

    def step(i, have):
        later_step = jnp.minimum(i + 1, twos - 1)
        have = fetch(have, listed[2 * later_step + 1] // 2 + 1)
        values = jnp.concatenate([vt[listed[2 * i]], vt[listed[2 * i + 1]]], axis=1)
        s = ahead[...]
        for h in range(HEADS):
            later = scores(i, h + 1) if h + 1 < HEADS else scores(later_step, 0)
            next_part(s, values, m.at[h], l.at[h], a.at[h])
            s = later
        ahead[...] = s
        return have

    def pairs(have):
        have = fetch(have, listed[1] // 2 + 1)
        ahead[...] = scores(0, 0)
        return lax.fori_loop(0, twos, step, have)

    have = lax.cond(twos > 0, pairs, lambda have: have, have)

    def single(have):
        last = listed[count - 1]
        have = fetch(have, last // 2 + 1)
        for h in range(HEADS):
            next_part(matmul_nt(k[last], q(h)), vt[last], m.at[h], l.at[h], a.at[h])
        return have

    return lax.cond(count % 2 == 1, single, lambda have: have, have)


def prefill_kernel(mask, q_ref, m, l, a, k_any, vt_any, o_ref, k, vt, ahead, listed, sems):
    chunks = k.shape[0] // 2

    def copies(i):
        two = pl.ds(2 * i, 2)
        return [
            pltpu.make_async_copy(k_any.at[two], k.at[two], sems.at[0, i]),
            pltpu.make_async_copy(vt_any.at[two], vt.at[two], sems.at[1, i]),
        ]

    def begin(i, carry):
        for c in copies(i):
            c.start()
        return carry

    def end(i, carry):
        for c in copies(i):
            c.wait()
        return carry

    def fetch(have, n):
        lax.fori_loop(have, n, end, 0)
        return jnp.maximum(have, n)

    lax.fori_loop(0, chunks, begin, 0)
    have = 0
    for b in range(2):
        rows = slice(b * BLK, (b + 1) * BLK)
        query = lambda h: q_ref[rows, h * D : (h + 1) * D]
        here = 2 * lax.axis_index("seq") + b
        have = prefill_block(
            here, mask, listed, query, m.at[b], l.at[b], a.at[b], k, vt, ahead, fetch, have
        )
        for h in range(HEADS):
            o_ref[rows, h * D : (h + 1) * D] = (a[b, h] / l[b, h]).T.astype(BF16)
    fetch(have, chunks)


def prefill(mask, q, m, l, a, k, vt):
    vmem = pl.BlockSpec(memory_space=pltpu.VMEM)
    anywhere = pl.BlockSpec(memory_space=pl.ANY)
    return pl.pallas_call(
        prefill_kernel,
        out_shape=jax.ShapeDtypeStruct(q.shape, BF16),
        in_specs=[pl.BlockSpec(memory_space=pltpu.SMEM)] + [vmem] * 4 + [anywhere] * 2,
        out_specs=vmem,
        scratch_shapes=[
            pltpu.VMEM(k.shape, BF16),
            pltpu.VMEM(vt.shape, BF16),
            pltpu.VMEM((2 * BLK, BLK), F32),
            pltpu.SMEM((40,), jnp.int32),
            pltpu.SemaphoreType.DMA((2, k.shape[0] // 2)),
        ],
        compiler_params=pltpu.CompilerParams(vmem_limit_bytes=56 << 20),
        cost_estimate=pl.CostEstimate(flops=40 * 10**9, bytes_accessed=10 << 20, transcendentals=16 << 20),
        name="prefill",
    )(mask, q, m, l, a, k, vt)


def body(prompt, w_query, key_weight, value_weight, q_gain, key_norm_gain, block_mask, tokens, row_map):
    here = prompt.shape[0]
    seq = lax.axis_index("seq")
    steps, rows, width = tokens.shape
    table = rope_tables(seq * here + jnp.arange(here))
    ttable = rope_tables(here * lax.axis_size("seq") + jnp.repeat(jnp.arange(steps), rows))
    q, m, l, a, decode_out, keys, values = front(
        prompt, w_query, key_weight, value_weight, tokens.reshape(steps * rows, width),
        q_gain[None], key_norm_gain[None], table, ttable, row_map[None],
    )
    return prefill(block_mask, q, m, l, a, keys, values), decode_out


def solution(mesh):
    return jax.shard_map(
        body,
        mesh=mesh,
        in_specs=(
            P("seq", None),
            P(None, "grp"),
            P(None, "grp"),
            P(None, "grp"),
            P(),
            P(),
            P(),
            P(None, "seq", None),
            P(),
        ),
        out_specs=(P("seq", "grp"), P(None, "grp", "seq")),
        check_vma=False,
    )
```

```python
import functools
import math

import jax
import jax.numpy as jnp
from jax import lax
from jax.experimental import pallas as pl
from jax.experimental.pallas import tpu as pltpu
from jax.sharding import PartitionSpec as P

HEADS = 4
D = 128
BLK = 512
ROPE_BASE = 1000000.0
NORM_EPS = 1e-06
SCALE = math.log2(math.e) / math.sqrt(D)
MASKED = -1e30
MESH = pl.DeviceIdType.MESH
F32, BF16 = jnp.float32, jnp.bfloat16


def rope_tables(positions):
    frequency = ROPE_BASE ** (-jnp.arange(D // 2, dtype=F32) * (2.0 / D))
    angles = positions.astype(F32)[:, None] * frequency[None, :]
    return jnp.concatenate([jnp.cos(angles), jnp.sin(angles)], axis=-1)


def both_halves(table):
    turned = pltpu.roll(table, D // 2, 1)
    low = lax.broadcasted_iota(jnp.int32, table.shape, 1) < D // 2
    return jnp.where(low, table, turned), jnp.where(low, -turned, table)


def norm_rope(u, gain, cosine, sine):
    normed = u * lax.rsqrt(jnp.mean(u * u, axis=-1, keepdims=True) + NORM_EPS) * gain
    return (normed * cosine + pltpu.roll(normed, D // 2, 1) * sine).astype(BF16)


def matmul(a, b):
    return lax.dot_general(a, b, (((1,), (0,)), ((), ())), preferred_element_type=F32)


def matmul_nt(a, b):
    return lax.dot_general(a, b, (((1,), (1,)), ((), ())), preferred_element_type=F32)


def front_kernel(
    x_any, wq_any, wk_any, wv_any, tok_any, qg_ref, kg_ref, table_ref, ttable_ref,
    q_ref, m, l, a, t_out, k_out, vt_out,
    x, wq, wkv, tok, k, vt, tall, load_sems, send_sems, recv_sems, store_sems,
):
    me, grp = lax.axis_index("seq"), lax.axis_index("grp")
    right, left = lax.rem(me + 4, 16), lax.rem(me + 12, 16)
    y = me + 2 - 4 * lax.rem(me // 2, 2)
    other_core = lambda s: s + 1 - 2 * lax.rem(s, 2)
    core = other_core(me)
    yright, yleft = lax.rem(y + 4, 16), lax.rem(y + 12, 16)
    far, yfar = lax.rem(me + 8, 16), lax.rem(y + 8, 16)
    barrier = pltpu.get_barrier_semaphore()
    for n in (right, left, y, core):
        pl.semaphore_signal(barrier, inc=1, device_id=(n, grp), device_id_type=MESH)
    pairs = [(wk_any, wkv.at[:, :D]), (wv_any, wkv.at[:, D:])]
    first, second = [(x_any.at[pl.ds(h * BLK, BLK)], x.at[pl.ds(h * BLK, BLK)]) for h in (0, 1)]
    pairs += [first, (tok_any, tok), (wq_any, wq), second]
    loads = [pltpu.make_async_copy(src, dst, load_sems.at[i]) for i, (src, dst) in enumerate(pairs)]
    for c in loads:
        c.start()

    sends = []
    outs = (k, vt, tall)
    K, V, T = 0, 1, 2

    def remote(kind, chunk, half, send_sem, to):
        block = outs[kind].at[2 * chunk + half]
        return pltpu.make_async_remote_copy(
            src_ref=block, dst_ref=block, send_sem=send_sem, recv_sem=recv_sems.at[kind, chunk, half],
            device_id=(to, grp), device_id_type=MESH,
        )

    def send(kind, chunk, half, to):
        c = remote(kind, chunk, half, send_sems.at[len(sends)], to)
        c.start()
        sends.append(c)

    def arrived(kind, chunk, half):
        remote(kind, chunk, half, send_sems.at[0], core).wait_recv()

    def forward(kind, chunk, half, *to):
        arrived(kind, chunk, half)
        for t in to:
            send(kind, chunk, half, t)

    n_tok = tok.shape[0]
    for h in (0, 1):
        for c in (loads[:3], loads[5:])[h]:
            c.wait()
        rows = slice(h * BLK, (h + 1) * BLK)
        kv = matmul(x[rows, :], wkv[...])
        cosine, sine = both_halves(table_ref[rows, :])
        k[2 * me + h] = norm_rope(kv[:, :D], kg_ref[...], cosine, sine)
        vt[2 * me + h] = kv[:, D:].T.astype(BF16)
        if h == 0:
            pl.semaphore_wait(barrier, 4)
        send(V, me, h, y)
        send(K, me, h, right)
        send(K, me, h, left)
        send(K, me, h, y)
        send(V, me, h, right)
        send(V, me, h, left)
        send(K, me, h, core)
        send(V, me, h, core)
        if h == 0:
            loads[3].wait()
            loads[4].wait()
            cosine, sine = both_halves(ttable_ref[...])
            kv = matmul(tok[...], wkv[...])
            q = matmul(tok[...], wq[...])
            mixed = [norm_rope(q[:, i * D : (i + 1) * D], qg_ref[...], cosine, sine) for i in range(HEADS)]
            mixed += [norm_rope(kv[:, :D], kg_ref[...], cosine, sine), kv[:, D:].astype(BF16)]
            mixed = jnp.concatenate(mixed, axis=1)
            for part in (0, 1):
                tall[2 * me + part] = mixed[part * n_tok // 2 : (part + 1) * n_tok // 2]
                for to in (y, right, left, core):
                    send(T, me, part, to)

    def query_tile(i):
        rows = slice(i * 256, (i + 1) * 256)
        cosine, sine = both_halves(table_ref[rows, :])
        q = matmul(x[rows, :], wq[...])
        for h in range(HEADS):
            cols = slice(h * D, (h + 1) * D)
            q_ref[rows, cols] = norm_rope(q[:, cols], qg_ref[...], cosine, sine)

    def diagonal(b):
        shape = (BLK, BLK)
        causal = lax.broadcasted_iota(jnp.int32, shape, 0) <= lax.broadcasted_iota(jnp.int32, shape, 1)
        for h in range(HEADS):
            s = matmul_nt(k[2 * me + b], q_ref[b * BLK : (b + 1) * BLK, h * D : (h + 1) * D])
            first_part(jnp.where(causal, s, MASKED), vt[2 * me + b], m.at[b, h], l.at[b, h], a.at[b, h])

    def store(chunk, i):
        two = pl.ds(2 * chunk, 2)
        return [
            pltpu.make_async_copy(k.at[two], k_out.at[two], store_sems.at[0, i]),
            pltpu.make_async_copy(vt.at[two], vt_out.at[two], store_sems.at[1, i]),
        ]

    order = (me, y, left, right, far, yleft, yright, yfar)

    def finish(i):
        for copy in store(order[i], 2 * i):
            copy.start()

    def finish_other(i):
        there = other_core(order[i])
        for kind in (K, V):
            for h in (0, 1):
                arrived(kind, there, h)
        for copy in store(there, 2 * i + 1):
            copy.start()

    forward(K, left, 0, right, y, core)
    forward(K, right, 0, y, core)
    forward(V, y, 0, right, left, core)
    query_tile(0)
    for h in (0, 1):
        forward(T, y, h, right, left, core)
    forward(K, right, 1, left, y, core)
    forward(K, left, 1, y, core)
    query_tile(1)
    forward(V, y, 1, right, left, core)
    forward(T, left, 0, right, core)
    forward(T, right, 1, left, core)
    forward(V, left, 0, right, core)
    query_tile(2)
    forward(V, right, 1, left, core)
    forward(K, far, 0, y, core)
    forward(T, left, 1, core)
    forward(T, right, 0, core)
    forward(V, left, 1, core)
    forward(V, right, 0, core)
    for h in (0, 1):
        forward(K, y, h, core)
    query_tile(3)
    forward(T, yleft, 0, right, core)
    forward(T, yright, 1, left, core)
    forward(K, far, 1, y, core)
    forward(V, yleft, 0, right, core)
    forward(V, yright, 1, left, core)
    diagonal(0)
    for i in range(4):
        finish(i)
    finish_other(0)
    finish_other(1)
    for h in (0, 1):
        forward(V, far, h, core)
    finish(4)
    finish_other(2)
    finish_other(3)
    for h in (0, 1):
        forward(K, yleft, h, core)
        forward(K, yright, 1 - h, core)
    forward(V, yleft, 1, core)
    forward(V, yright, 0, core)
    finish(5)
    finish(6)
    forward(T, yleft, 1, core)
    forward(T, yright, 0, core)
    for h in (0, 1):
        forward(T, far, h, core)
    diagonal(1)
    for h in (0, 1):
        forward(K, yfar, h, core)
        forward(V, yfar, h, core)
    finish(7)
    for h in (0, 1):
        forward(T, yfar, h, core)
    for i in range(4, 8):
        finish_other(i)
    for chunk in order:
        for h in (0, 1):
            arrived(T, other_core(chunk), h)
    last = pltpu.make_async_copy(tall, t_out, load_sems.at[0])
    last.start()
    for c in sends:
        c.wait_send()
    for i in range(8):
        for c in store(order[i], 2 * i) + store(other_core(order[i]), 2 * i + 1):
            c.wait()
    last.wait()


def front(x, wq, wk, wv, tok, qg, kg, table, ttable):
    rows, width = x.shape
    n_tok = tok.shape[0]
    vmem = pl.BlockSpec(memory_space=pltpu.VMEM)
    anywhere = pl.BlockSpec(memory_space=pl.ANY)
    dma = pltpu.SemaphoreType.DMA
    mixed = (32, n_tok // 2, (HEADS + 2) * D)
    return pl.pallas_call(
        front_kernel,
        out_shape=[
            jax.ShapeDtypeStruct((rows, HEADS * D), BF16),
            jax.ShapeDtypeStruct((2, HEADS, 1, BLK), F32),
            jax.ShapeDtypeStruct((2, HEADS, 1, BLK), F32),
            jax.ShapeDtypeStruct((2, HEADS, D, BLK), F32),
            jax.ShapeDtypeStruct(mixed, BF16),
            jax.ShapeDtypeStruct((32, BLK, D), BF16),
            jax.ShapeDtypeStruct((32, D, BLK), BF16),
        ],
        in_specs=[anywhere] * 5 + [vmem] * 4,
        out_specs=[vmem] * 4 + [anywhere] * 3,
        scratch_shapes=[
            pltpu.VMEM((rows, width), BF16),
            pltpu.VMEM((width, HEADS * D), BF16),
            pltpu.VMEM((width, 2 * D), BF16),
            pltpu.VMEM((n_tok, width), BF16),
            pltpu.VMEM((32, BLK, D), BF16),
            pltpu.VMEM((32, D, BLK), BF16),
            pltpu.VMEM(mixed, BF16),
            dma((6,)),
            dma((96,)),
            dma((3, 16, 2)),
            dma((2, 16)),
        ],
        compiler_params=pltpu.CompilerParams(
            collective_id=0, has_side_effects=True, vmem_limit_bytes=60 << 20
        ),
        name="front",
    )(x, wq, wk, wv, tok, qg, kg, table, ttable)


def first_part(s, vt, m, l, a):
    top = jnp.max(s, axis=0, keepdims=True)
    p = jnp.exp2((s - top) * SCALE)
    m[...] = top
    l[...] = jnp.sum(p, axis=0, keepdims=True)
    a[...] = matmul(vt, p.astype(BF16))


def next_part(s, vt, m, l, a):
    before = m[...]
    top = jnp.maximum(before, jnp.max(s, axis=0, keepdims=True))
    p = jnp.exp2(s * SCALE - top * SCALE)
    keep = jnp.exp2((before - top) * SCALE)
    l[...] = l[...] * keep + jnp.sum(p, axis=0, keepdims=True)
    a[...] = a[...] * keep + matmul(vt, p.astype(BF16))
    m[...] = top


def prefill_block(here, mask, listed, q, m, l, a, k, vt, ahead, fetch, have):
    listed[0] = 0

    def note(j, n):
        listed[n] = j
        return n + jnp.where(mask[here, j] > 0, 1, 0)

    count = lax.fori_loop(0, here, note, 0)
    fours = count // 4

    def keys(first, n):
        return jnp.concatenate([k[listed[first + j]] for j in range(n)], axis=0)

    def values(first, n):
        return jnp.concatenate([vt[listed[first + j]] for j in range(n)], axis=1)

    def step(i, have):
        later_step = jnp.minimum(i + 1, fours - 1)
        have = fetch(have, listed[4 * later_step + 3] // 2 + 1)
        vs = values(4 * i, 4)
        s = ahead[...]
        for h in range(HEADS):
            later = matmul_nt(keys(4 * i, 4), q(h + 1)) if h + 1 < HEADS else matmul_nt(keys(4 * later_step, 4), q(0))
            next_part(s, vs, m.at[h], l.at[h], a.at[h])
            s = later
        ahead[...] = s
        return have

    def many(have):
        have = fetch(have, listed[3] // 2 + 1)
        ahead[...] = matmul_nt(keys(0, 4), q(0))
        return lax.fori_loop(0, fours, step, have)

    have = lax.cond(fours > 0, many, lambda have: have, have)

    def few(first, n, have):
        have = fetch(have, listed[first + n - 1] // 2 + 1)
        ks, vs = keys(first, n), values(first, n)
        later = matmul_nt(ks, q(0))
        for h in range(HEADS):
            s = later
            if h + 1 < HEADS:
                later = matmul_nt(ks, q(h + 1))
            next_part(s, vs, m.at[h], l.at[h], a.at[h])
        return have

    have = lax.cond(count % 4 >= 2, lambda have: few(4 * fours, 2, have), lambda have: have, have)
    return lax.cond(count % 2 == 1, lambda have: few(count - 1, 1, have), lambda have: have, have)


def slot_rows(map_ref, mixed, tq):
    steps, per, here = 4, 32, 16
    n = steps * per
    shape = (n, map_ref.shape[1])
    slot = lax.axis_index("seq") * per + lax.broadcasted_iota(jnp.int32, shape, 0) % per
    mine = lax.broadcasted_iota(jnp.int32, shape, 1) == slot
    row = jnp.sum(jnp.where(mine, map_ref[...].astype(F32), 0.0), axis=1, keepdims=True).astype(jnp.int32)
    step = lax.broadcasted_iota(jnp.int32, (n, 1), 0) // per
    source = (row >> 4) * (steps * here) + step * here + (row & 15)
    shape = (n, 16 * steps * here)
    picked = jnp.where(lax.broadcasted_iota(jnp.int32, shape, 1) == source, 1.0, 0.0).astype(BF16)
    rows = matmul(picked, mixed[...].reshape(shape[1], (HEADS + 2) * D))
    for h in range(HEADS):
        tq[h * n : (h + 1) * n, :] = rows[:, h * D : (h + 1) * D].astype(BF16)
    return rows[:, HEADS * D : (HEADS + 1) * D].astype(BF16), rows[:, (HEADS + 1) * D :].T.astype(BF16)


def own_step_scores(tk, tq):
    per = 32
    n_tok = tk.shape[0]
    own = matmul_nt(tk, tq[...])
    key_id = lax.broadcasted_iota(jnp.int32, own.shape, 0)
    row_id = lax.broadcasted_iota(jnp.int32, own.shape, 1) % n_tok
    seen = (key_id % per == row_id % per) & (key_id // per <= row_id // per)
    return jnp.where(seen, own, MASKED)


def prefill_kernel(
    mask, q_ref, m, l, a, map_ref, mixed, k_any, vt_any, o_ref, rows_ref,
    k, vt, ahead, listed, sems, tq, tm, tl, ta, have_ref,
):
    chunks = k.shape[0] // 2

    def copies(i):
        two = pl.ds(2 * i, 2)
        return [
            pltpu.make_async_copy(k_any.at[two], k.at[two], sems.at[0, i]),
            pltpu.make_async_copy(vt_any.at[two], vt.at[two], sems.at[1, i]),
        ]

    def begin(i, carry):
        for c in copies(i):
            c.start()
        return carry

    def end(i, carry):
        for c in copies(i):
            c.wait()
        return carry

    def fetch(have, n):
        lax.fori_loop(have, n, end, 0)
        return jnp.maximum(have, n)

    lax.fori_loop(0, chunks, begin, 0)
    seq = lax.axis_index("seq")
    have_ref[0] = 0

    @pl.when(seq < 8)
    def _():
        tk, tvt = slot_rows(map_ref, mixed, tq)
        first_part(own_step_scores(tk, tq), tvt, tm, tl, ta)
        keys = lambda i: jnp.concatenate([k[4 * i + j] for j in range(4)], axis=0)
        have = fetch(0, 2)
        ahead[...] = matmul_nt(keys(0), tq[...])

        def step(i, have):
            later_step = jnp.minimum(i + 1, chunks // 2 - 1)
            have = fetch(have, 2 * later_step + 2)
            s = ahead[...]
            later = matmul_nt(keys(later_step), tq[...])
            next_part(s, jnp.concatenate([vt[4 * i + j] for j in range(4)], axis=1), tm, tl, ta)
            ahead[...] = later
            return have

        have_ref[0] = lax.fori_loop(0, chunks // 2, step, have)
        out = (ta[...] / tl[...]).T.astype(BF16)
        n = out.shape[0] // HEADS
        for h in range(HEADS):
            rows_ref[h // 2, :, h % 2 * D : (h % 2 + 1) * D] = out[h * n : (h + 1) * n, :]

    have = have_ref[0]
    for b in range(2):
        rows = slice(b * BLK, (b + 1) * BLK)
        query = lambda h: q_ref[rows, h * D : (h + 1) * D]
        here = 2 * seq + b
        have = prefill_block(
            here, mask, listed, query, m.at[b], l.at[b], a.at[b], k, vt, ahead, fetch, have
        )
        for h in range(HEADS):
            o_ref[rows, h * D : (h + 1) * D] = (a[b, h] / l[b, h]).T.astype(BF16)
    fetch(have, chunks)


def prefill(mask, q, m, l, a, row_map, mixed, k, vt):
    vmem = pl.BlockSpec(memory_space=pltpu.VMEM)
    anywhere = pl.BlockSpec(memory_space=pl.ANY)
    n = 128
    return pl.pallas_call(
        prefill_kernel,
        out_shape=[jax.ShapeDtypeStruct(q.shape, BF16), jax.ShapeDtypeStruct((2, n, 2 * D), BF16)],
        in_specs=[pl.BlockSpec(memory_space=pltpu.SMEM)] + [vmem] * 6 + [anywhere] * 2,
        out_specs=[vmem] * 2,
        scratch_shapes=[
            pltpu.VMEM(k.shape, BF16),
            pltpu.VMEM(vt.shape, BF16),
            pltpu.VMEM((4 * BLK, BLK), F32),
            pltpu.SMEM((40,), jnp.int32),
            pltpu.SemaphoreType.DMA((2, k.shape[0] // 2)),
            pltpu.VMEM((HEADS * n, D), BF16),
            pltpu.VMEM((1, HEADS * n), F32),
            pltpu.VMEM((1, HEADS * n), F32),
            pltpu.VMEM((D, HEADS * n), F32),
            pltpu.SMEM((1,), jnp.int32),
        ],
        compiler_params=pltpu.CompilerParams(vmem_limit_bytes=60 << 20),
        cost_estimate=pl.CostEstimate(flops=40 * 10**9, bytes_accessed=10 << 20, transcendentals=16 << 20),
        name="prefill",
    )(mask, q, m, l, a, row_map, mixed, k, vt)


def place_kernel(rows_ref, o_ref, landing, send_sems, recv_sem):
    me, grp = lax.axis_index("seq"), lax.axis_index("grp")
    sender = (grp, me // 2)
    from_here = (grp == me) & (me // 2 == grp)
    barrier = pltpu.get_barrier_semaphore()

    @pl.when(jnp.logical_not(from_here))
    def _():
        pl.semaphore_signal(barrier, inc=1, device_id=sender, device_id_type=MESH)

    def stays(c):
        return (me == 2 * grp + c) & (grp == me)

    def send(c):
        return pltpu.make_async_remote_copy(
            src_ref=rows_ref.at[c], dst_ref=landing, send_sem=send_sems.at[c], recv_sem=recv_sem.at[0],
            device_id=(2 * grp + c, me), device_id_type=MESH,
        )

    @pl.when(me < 8)
    def _():
        pl.semaphore_wait(barrier, 2 - jnp.where(from_here, 1, 0))
        for c in (0, 1):
            pl.when(jnp.logical_not(stays(c)))(lambda c=c: send(c).start())

    @pl.when(from_here)
    def _():
        own = pltpu.make_async_copy(rows_ref.at[0], landing, recv_sem.at[0])
        own.start()
        own.wait()

    @pl.when(jnp.logical_not(from_here))
    def _():
        pltpu.make_async_remote_copy(
            src_ref=landing, dst_ref=landing, send_sem=send_sems.at[0], recv_sem=recv_sem.at[0],
            device_id=sender, device_id_type=MESH,
        ).wait_recv()

    steps, slots = o_ref.shape[:2]
    for t in range(steps):
        o_ref[t] = landing[t * slots : (t + 1) * slots, :]

    @pl.when(me < 8)
    def _():
        for c in (0, 1):
            pl.when(jnp.logical_not(stays(c)))(lambda c=c: send(c).wait_send())


def place(rows, steps):
    n, cols = rows.shape[1:]
    vmem = pl.BlockSpec(memory_space=pltpu.VMEM)
    return pl.pallas_call(
        place_kernel,
        out_shape=jax.ShapeDtypeStruct((steps, n // steps, cols), BF16),
        in_specs=[vmem],
        out_specs=vmem,
        scratch_shapes=[
            pltpu.VMEM((n, cols), BF16),
            pltpu.SemaphoreType.DMA((2,)),
            pltpu.SemaphoreType.DMA((1,)),
        ],
        compiler_params=pltpu.CompilerParams(collective_id=1, has_side_effects=True),
        name="place",
    )(rows)


def body(prompt, w_query, key_weight, value_weight, q_gain, key_norm_gain, block_mask, tokens, row_map):
    here = prompt.shape[0]
    seq = lax.axis_index("seq")
    steps, rows, width = tokens.shape
    table = rope_tables(seq * here + jnp.arange(here))
    ttable = rope_tables(here * lax.axis_size("seq") + jnp.repeat(jnp.arange(steps), rows))
    q, m, l, a, mixed, keys, values = front(
        prompt, w_query, key_weight, value_weight, tokens.reshape(steps * rows, width),
        q_gain[None], key_norm_gain[None], table, ttable,
    )
    prefill_out, rows_out = prefill(block_mask, q, m, l, a, row_map[None], mixed, keys, values)
    return prefill_out, place(rows_out, steps)


def solution(mesh):
    return jax.shard_map(
        body,
        mesh=mesh,
        in_specs=(
            P("seq", None),
            P(None, "grp"),
            P(None, "grp"),
            P(None, "grp"),
            P(),
            P(),
            P(),
            P(None, "seq", None),
            P(),
        ),
        out_specs=(P("seq", "grp"), P(None, "grp", "seq")),
        check_vma=False,
    )
```

```python
import functools
import math

import jax
import jax.numpy as jnp
from jax import lax
from jax.experimental import pallas as pl
from jax.experimental.pallas import tpu as pltpu
from jax.sharding import PartitionSpec as P

HEADS = 4
D = 128
BLK = 512
ROPE_BASE = 1000000.0
NORM_EPS = 1e-06
SCALE = math.log2(math.e) / math.sqrt(D)
MASKED = -1e30
MESH = pl.DeviceIdType.MESH
F32, BF16 = jnp.float32, jnp.bfloat16


def rope_tables(positions):
    frequency = ROPE_BASE ** (-jnp.arange(D // 2, dtype=F32) * (2.0 / D))
    angles = positions.astype(F32)[:, None] * frequency[None, :]
    return jnp.concatenate([jnp.cos(angles), jnp.sin(angles)], axis=-1)


def both_halves(table):
    turned = pltpu.roll(table, D // 2, 1)
    low = lax.broadcasted_iota(jnp.int32, table.shape, 1) < D // 2
    return jnp.where(low, table, turned), jnp.where(low, -turned, table)


def norm_rope(u, gain, cosine, sine):
    normed = u * lax.rsqrt(jnp.mean(u * u, axis=-1, keepdims=True) + NORM_EPS) * gain
    return (normed * cosine + pltpu.roll(normed, D // 2, 1) * sine).astype(BF16)


def matmul(a, b):
    return lax.dot_general(a, b, (((1,), (0,)), ((), ())), preferred_element_type=F32)


def matmul_nt(a, b):
    return lax.dot_general(a, b, (((1,), (1,)), ((), ())), preferred_element_type=F32)


def front_kernel(
    x_any, wq_any, wk_any, wv_any, tok_any, qg_ref, kg_ref, table_ref, ttable_ref, map_ref,
    q_ref, m, l, a, decode_ref, k_out, vt_out,
    x, wq, wkv, tok, k, vt, tq, tm, tl, ta, rows_out, arriving, tall, load_sems, send_sems, recv_sems, store_sems,
    out_sems, in_sems,
):
    me, grp = lax.axis_index("seq"), lax.axis_index("grp")
    right, left = lax.rem(me + 4, 16), lax.rem(me + 12, 16)
    y = me + 2 - 4 * lax.rem(me // 2, 2)
    other_core = lambda s: s + 1 - 2 * lax.rem(s, 2)
    core = other_core(me)
    yright, yleft = lax.rem(y + 4, 16), lax.rem(y + 12, 16)
    far, yfar = lax.rem(me + 8, 16), lax.rem(y + 8, 16)
    barrier = pltpu.get_barrier_semaphore()
    for n in (right, left, y, core):
        pl.semaphore_signal(barrier, inc=1, device_id=(n, grp), device_id_type=MESH)
    home = me // 2
    at_home = home == grp

    def is_me(c):
        return at_home & (2 * grp + c == me)

    for c in (0, 1):

        @pl.when(jnp.logical_not(is_me(c)))
        def _():
            pl.semaphore_signal(barrier, inc=1, device_id=(2 * grp + c, home), device_id_type=MESH)

    pairs = [(wk_any, wkv.at[:, :D]), (wv_any, wkv.at[:, D:])]
    pairs += [(tok_any, tok), (wq_any, wq)]
    pairs += [(x_any.at[pl.ds(h * BLK, BLK)], x.at[pl.ds(h * BLK, BLK)]) for h in (0, 1)]
    loads = [pltpu.make_async_copy(src, dst, load_sems.at[i]) for i, (src, dst) in enumerate(pairs)]
    for c in loads:
        c.start()

    sends = []
    outs = (k, vt, tall)
    K, V, T = 0, 1, 2

    def remote(kind, chunk, half, send_sem, to):
        block = outs[kind].at[2 * chunk + half]
        return pltpu.make_async_remote_copy(
            src_ref=block, dst_ref=block, send_sem=send_sem, recv_sem=recv_sems.at[kind, chunk, half],
            device_id=(to, grp), device_id_type=MESH,
        )

    def send(kind, chunk, half, to):
        c = remote(kind, chunk, half, send_sems.at[len(sends)], to)
        c.start()
        sends.append(c)

    def arrived(kind, chunk, half):
        remote(kind, chunk, half, send_sems.at[0], core).wait_recv()

    def forward(kind, chunk, half, *to):
        arrived(kind, chunk, half)
        for t in to:
            send(kind, chunk, half, t)

    n_tok = tok.shape[0]
    steps = 4
    per = n_tok // steps
    for c in loads[:4]:
        c.wait()
    cosine, sine = both_halves(ttable_ref[...])
    kv = matmul(tok[...], wkv[...])
    q = matmul(tok[...], wq[...])
    mixed = [norm_rope(q[:, h * D : (h + 1) * D], qg_ref[...], cosine, sine) for h in range(HEADS)]
    mixed += [norm_rope(kv[:, :D], kg_ref[...], cosine, sine), kv[:, D:].astype(BF16)]
    mixed = jnp.concatenate(mixed, axis=1)
    for h in (0, 1):
        tall[2 * me + h] = mixed[h * n_tok // 2 : (h + 1) * n_tok // 2]
    pl.semaphore_wait(barrier, 6 - jnp.where(at_home, 1, 0))
    for h in (0, 1):
        for to in (y, right, left, core):
            send(T, me, h, to)
    for h in (0, 1):
        loads[4 + h].wait()
        rows = slice(h * BLK, (h + 1) * BLK)
        kv = matmul(x[rows, :], wkv[...])
        cosine, sine = both_halves(table_ref[rows, :])
        k[2 * me + h] = norm_rope(kv[:, :D], kg_ref[...], cosine, sine)
        vt[2 * me + h] = kv[:, D:].T.astype(BF16)
        send(V, me, h, y)
        send(K, me, h, right)
        send(K, me, h, left)
        send(K, me, h, y)
        send(V, me, h, right)
        send(V, me, h, left)
        send(K, me, h, core)
        send(V, me, h, core)

    def query_tile(i):
        rows = slice(i * 256, (i + 1) * 256)
        cosine, sine = both_halves(table_ref[rows, :])
        q = matmul(x[rows, :], wq[...])
        for h in range(HEADS):
            cols = slice(h * D, (h + 1) * D)
            q_ref[rows, cols] = norm_rope(q[:, cols], qg_ref[...], cosine, sine)

    def slots():
        shape = (n_tok, map_ref.shape[1])
        slot = me * per + lax.broadcasted_iota(jnp.int32, shape, 0) % per
        mine = lax.broadcasted_iota(jnp.int32, shape, 1) == slot
        row = jnp.sum(jnp.where(mine, map_ref[...].astype(F32), 0.0), axis=1, keepdims=True).astype(jnp.int32)
        source = (row >> 4) * n_tok + lax.broadcasted_iota(jnp.int32, (n_tok, 1), 0) // per * per + (row & 15)
        shape = (n_tok, 16 * n_tok)
        picked = jnp.where(lax.broadcasted_iota(jnp.int32, shape, 1) == source, 1.0, 0.0).astype(BF16)
        mixed = matmul(picked, tall[...].reshape(16 * n_tok, (HEADS + 2) * D))
        for h in range(HEADS):
            tq[h * n_tok : (h + 1) * n_tok, :] = mixed[:, h * D : (h + 1) * D].astype(BF16)
        tk = mixed[:, HEADS * D : (HEADS + 1) * D].astype(BF16)
        tvt = mixed[:, (HEADS + 1) * D :].T.astype(BF16)
        own = matmul_nt(tk, tq[...])
        key_id = lax.broadcasted_iota(jnp.int32, own.shape, 0)
        row_id = lax.broadcasted_iota(jnp.int32, own.shape, 1) % n_tok
        seen = (key_id % per == row_id % per) & (key_id // per <= row_id // per)
        first_part(jnp.where(seen, own, MASKED), tvt, tm, tl, ta)

    def diagonal(b):
        shape = (BLK, BLK)
        causal = lax.broadcasted_iota(jnp.int32, shape, 0) <= lax.broadcasted_iota(jnp.int32, shape, 1)
        for h in range(HEADS):
            s = matmul_nt(k[2 * me + b], q_ref[b * BLK : (b + 1) * BLK, h * D : (h + 1) * D])
            first_part(jnp.where(causal, s, MASKED), vt[2 * me + b], m.at[b, h], l.at[b, h], a.at[b, h])

    def store(chunk, i):
        two = pl.ds(2 * chunk, 2)
        return [
            pltpu.make_async_copy(k.at[two], k_out.at[two], store_sems.at[0, i]),
            pltpu.make_async_copy(vt.at[two], vt_out.at[two], store_sems.at[1, i]),
        ]

    def chunk_of(base, dx, c):
        mine = lax.rem(base + 4 * dx, 16)
        return mine if c == 0 else other_core(mine)

    def decode(base, first):
        def step(dx, carry):
            here, there = chunk_of(base, dx, 0), chunk_of(base, dx, 1)
            for kind in (K, V):
                for h in (0, 1):
                    arrived(kind, there, h)
            scores = [
                matmul_nt(jnp.concatenate([k[2 * c], k[2 * c + 1]], axis=0), tq[...]) for c in (here, there)
            ]
            for s, c, i in zip(scores, (here, there), (0, 1)):
                for copy in store(c, first + 2 * dx + i):
                    copy.start()
                next_part(s, jnp.concatenate([vt[2 * c], vt[2 * c + 1]], axis=1), tm, tl, ta)
            return carry

        lax.fori_loop(0, 4, step, 0)

    for h in (0, 1):
        forward(T, y, h, right, left, core)
    forward(T, left, 0, right, core)
    forward(T, right, 1, left, core)
    forward(K, left, 0, right, y, core)
    forward(K, right, 0, y, core)
    for h in (0, 1):
        forward(V, y, h, right, left, core)
    forward(T, left, 1, core)
    forward(T, right, 0, core)
    forward(T, yleft, 0, right, core)
    forward(T, yright, 1, left, core)
    query_tile(0)
    forward(K, right, 1, left, y, core)
    forward(K, left, 1, y, core)
    forward(V, left, 0, right, core)
    forward(T, yleft, 1, core)
    forward(T, yright, 0, core)
    for h in (0, 1):
        forward(T, far, h, core)
    query_tile(1)
    forward(V, right, 0, core)
    forward(V, right, 1, left, core)
    forward(V, left, 1, core)
    for h in (0, 1):
        forward(T, yfar, h, core)
    query_tile(2)
    for h in (0, 1):
        forward(K, y, h, core)
    forward(K, far, 0, y, core)
    query_tile(3)
    for chunk in (me, y, left, right, far, yleft, yright, yfar):
        for h in (0, 1):
            arrived(T, other_core(chunk), h)
    slots()
    forward(K, far, 1, y, core)
    forward(V, yleft, 0, right, core)
    forward(V, yright, 1, left, core)
    for h in (0, 1):
        forward(V, far, h, core)
    for h in (0, 1):
        forward(K, yleft, h, core)
        forward(K, yright, 1 - h, core)
    forward(V, yleft, 1, core)
    forward(V, yright, 0, core)
    decode(me, 0)
    for h in (0, 1):
        forward(K, yfar, h, core)
        forward(V, yfar, h, core)
    decode(y, 8)
    out = (ta[...] / tl[...]).T.astype(BF16)
    for c in (0, 1):
        for h in (0, 1):
            rows = slice((2 * c + h) * n_tok, (2 * c + h + 1) * n_tok)
            rows_out[c, :, h * D : (h + 1) * D] = out[rows, :]

    def place(c):
        here = arriving.at[lax.rem(me, 2)]
        local = pltpu.make_async_copy(rows_out.at[c], here, out_sems.at[c])
        away = pltpu.make_async_remote_copy(
            src_ref=rows_out.at[c], dst_ref=here, send_sem=out_sems.at[c], recv_sem=in_sems.at[lax.rem(me, 2)],
            device_id=(2 * grp + c, home), device_id_type=MESH,
        )
        return local, away

    for c in (0, 1):
        local, away = place(c)
        pl.when(is_me(c))(local.start)
        pl.when(jnp.logical_not(is_me(c)))(away.start)
    diagonal(0)
    diagonal(1)
    for c in (0, 1):
        local, away = place(c)
        pl.when(is_me(c))(local.wait)
        pl.when(jnp.logical_not(is_me(c)))(away.wait_send)
        there = pltpu.make_async_remote_copy(
            src_ref=arriving.at[c], dst_ref=arriving.at[c], send_sem=out_sems.at[c], recv_sem=in_sems.at[c],
            device_id=(core, grp), device_id_type=MESH,
        )
        pl.when(jnp.logical_not(is_me(c)))(there.wait_recv)
    for t in range(steps):
        for c in (0, 1):
            decode_ref[t, c * per : (c + 1) * per, :] = arriving[c, t * per : (t + 1) * per, :]
    for c in sends:
        c.wait_send()
    for base, first in ((me, 0), (y, 8)):

        def finish(dx, carry):
            for i in (0, 1):
                for copy in store(chunk_of(base, dx, i), first + 2 * dx + i):
                    copy.wait()
            return carry

        lax.fori_loop(0, 4, finish, 0)


def front(x, wq, wk, wv, tok, qg, kg, table, ttable, row_map):
    rows, width = x.shape
    n_tok = tok.shape[0]
    vmem = pl.BlockSpec(memory_space=pltpu.VMEM)
    anywhere = pl.BlockSpec(memory_space=pl.ANY)
    dma = pltpu.SemaphoreType.DMA
    return pl.pallas_call(
        front_kernel,
        out_shape=[
            jax.ShapeDtypeStruct((rows, HEADS * D), BF16),
            jax.ShapeDtypeStruct((2, HEADS, 1, BLK), F32),
            jax.ShapeDtypeStruct((2, HEADS, 1, BLK), F32),
            jax.ShapeDtypeStruct((2, HEADS, D, BLK), F32),
            jax.ShapeDtypeStruct((4, n_tok // 2, 2 * D), BF16),
            jax.ShapeDtypeStruct((32, BLK, D), BF16),
            jax.ShapeDtypeStruct((32, D, BLK), BF16),
        ],
        in_specs=[anywhere] * 5 + [vmem] * 5,
        out_specs=[vmem] * 5 + [anywhere] * 2,
        scratch_shapes=[
            pltpu.VMEM((rows, width), BF16),
            pltpu.VMEM((width, HEADS * D), BF16),
            pltpu.VMEM((width, 2 * D), BF16),
            pltpu.VMEM((n_tok, width), BF16),
            pltpu.VMEM((32, BLK, D), BF16),
            pltpu.VMEM((32, D, BLK), BF16),
            pltpu.VMEM((HEADS * n_tok, D), BF16),
            pltpu.VMEM((1, HEADS * n_tok), F32),
            pltpu.VMEM((1, HEADS * n_tok), F32),
            pltpu.VMEM((D, HEADS * n_tok), F32),
            pltpu.VMEM((2, n_tok, 2 * D), BF16),
            pltpu.VMEM((2, n_tok, 2 * D), BF16),
            pltpu.VMEM((32, n_tok // 2, (HEADS + 2) * D), BF16),
            dma((6,)),
            dma((96,)),
            dma((3, 16, 2)),
            dma((2, 16)),
            dma((2,)),
            dma((2,)),
        ],
        compiler_params=pltpu.CompilerParams(
            collective_id=0, has_side_effects=True, vmem_limit_bytes=56 << 20
        ),
        name="front",
    )(x, wq, wk, wv, tok, qg, kg, table, ttable, row_map)


def first_part(s, vt, m, l, a):
    top = jnp.max(s, axis=0, keepdims=True)
    p = jnp.exp2((s - top) * SCALE)
    m[...] = top
    l[...] = jnp.sum(p, axis=0, keepdims=True)
    a[...] = matmul(vt, p.astype(BF16))


def next_part(s, vt, m, l, a):
    before = m[...]
    top = jnp.maximum(before, jnp.max(s, axis=0, keepdims=True))
    p = jnp.exp2(s * SCALE - top * SCALE)
    keep = jnp.exp2((before - top) * SCALE)
    l[...] = l[...] * keep + jnp.sum(p, axis=0, keepdims=True)
    a[...] = a[...] * keep + matmul(vt, p.astype(BF16))
    m[...] = top


def prefill_block(here, mask, listed, q, m, l, a, k, vt, ahead, fetch, have):
    listed[0] = 0

    def note(j, n):
        listed[n] = j
        return n + jnp.where(mask[here, j] > 0, 1, 0)

    count = lax.fori_loop(0, here, note, 0)
    fours = count // 4

    def keys(first, n):
        return jnp.concatenate([k[listed[first + j]] for j in range(n)], axis=0)

    def values(first, n):
        return jnp.concatenate([vt[listed[first + j]] for j in range(n)], axis=1)

    def step(i, have):
        later_step = jnp.minimum(i + 1, fours - 1)
        have = fetch(have, listed[4 * later_step + 3] // 2 + 1)
        vs = values(4 * i, 4)
        s = ahead[...]
        for h in range(HEADS):
            later = matmul_nt(keys(4 * i, 4), q(h + 1)) if h + 1 < HEADS else matmul_nt(keys(4 * later_step, 4), q(0))
            next_part(s, vs, m.at[h], l.at[h], a.at[h])
            s = later
        ahead[...] = s
        return have

    def many(have):
        have = fetch(have, listed[3] // 2 + 1)
        ahead[...] = matmul_nt(keys(0, 4), q(0))
        return lax.fori_loop(0, fours, step, have)

    have = lax.cond(fours > 0, many, lambda have: have, have)

    def few(first, n, have):
        have = fetch(have, listed[first + n - 1] // 2 + 1)
        ks, vs = keys(first, n), values(first, n)
        later = matmul_nt(ks, q(0))
        for h in range(HEADS):
            s = later
            if h + 1 < HEADS:
                later = matmul_nt(ks, q(h + 1))
            next_part(s, vs, m.at[h], l.at[h], a.at[h])
        return have

    have = lax.cond(count % 4 >= 2, lambda have: few(4 * fours, 2, have), lambda have: have, have)
    return lax.cond(count % 2 == 1, lambda have: few(count - 1, 1, have), lambda have: have, have)


def prefill_kernel(mask, q_ref, m, l, a, k_any, vt_any, o_ref, k, vt, ahead, listed, sems):
    chunks = k.shape[0] // 2

    def copies(i):
        two = pl.ds(2 * i, 2)
        return [
            pltpu.make_async_copy(k_any.at[two], k.at[two], sems.at[0, i]),
            pltpu.make_async_copy(vt_any.at[two], vt.at[two], sems.at[1, i]),
        ]

    def begin(i, carry):
        for c in copies(i):
            c.start()
        return carry

    def end(i, carry):
        for c in copies(i):
            c.wait()
        return carry

    def fetch(have, n):
        lax.fori_loop(have, n, end, 0)
        return jnp.maximum(have, n)

    lax.fori_loop(0, chunks, begin, 0)
    have = 0
    for b in range(2):
        rows = slice(b * BLK, (b + 1) * BLK)
        query = lambda h: q_ref[rows, h * D : (h + 1) * D]
        here = 2 * lax.axis_index("seq") + b
        have = prefill_block(
            here, mask, listed, query, m.at[b], l.at[b], a.at[b], k, vt, ahead, fetch, have
        )
        for h in range(HEADS):
            o_ref[rows, h * D : (h + 1) * D] = (a[b, h] / l[b, h]).T.astype(BF16)
    fetch(have, chunks)


def prefill(mask, q, m, l, a, k, vt):
    vmem = pl.BlockSpec(memory_space=pltpu.VMEM)
    anywhere = pl.BlockSpec(memory_space=pl.ANY)
    return pl.pallas_call(
        prefill_kernel,
        out_shape=jax.ShapeDtypeStruct(q.shape, BF16),
        in_specs=[pl.BlockSpec(memory_space=pltpu.SMEM)] + [vmem] * 4 + [anywhere] * 2,
        out_specs=vmem,
        scratch_shapes=[
            pltpu.VMEM(k.shape, BF16),
            pltpu.VMEM(vt.shape, BF16),
            pltpu.VMEM((4 * BLK, BLK), F32),
            pltpu.SMEM((40,), jnp.int32),
            pltpu.SemaphoreType.DMA((2, k.shape[0] // 2)),
        ],
        compiler_params=pltpu.CompilerParams(vmem_limit_bytes=56 << 20),
        cost_estimate=pl.CostEstimate(flops=40 * 10**9, bytes_accessed=10 << 20, transcendentals=16 << 20),
        name="prefill",
    )(mask, q, m, l, a, k, vt)


def body(prompt, w_query, key_weight, value_weight, q_gain, key_norm_gain, block_mask, tokens, row_map):
    here = prompt.shape[0]
    seq = lax.axis_index("seq")
    steps, rows, width = tokens.shape
    table = rope_tables(seq * here + jnp.arange(here))
    ttable = rope_tables(here * lax.axis_size("seq") + jnp.repeat(jnp.arange(steps), rows))
    q, m, l, a, decode_out, keys, values = front(
        prompt, w_query, key_weight, value_weight, tokens.reshape(steps * rows, width),
        q_gain[None], key_norm_gain[None], table, ttable, row_map[None],
    )
    return prefill(block_mask, q, m, l, a, keys, values), decode_out


def solution(mesh):
    return jax.shard_map(
        body,
        mesh=mesh,
        in_specs=(
            P("seq", None),
            P(None, "grp"),
            P(None, "grp"),
            P(None, "grp"),
            P(),
            P(),
            P(),
            P(None, "seq", None),
            P(),
        ),
        out_specs=(P("seq", "grp"), P(None, "grp", "seq")),
        check_vma=False,
    )
```
